512 devices in a mesh: dp: 64 (over y_lo, z, core), fsdp: 8 (over y_hi, x).
Axes of the slice: x: 4, y: 4 (y_hi: 2, y_lo: 2; y = y_hi * 2 + y_lo), z: 16, core: 2. Of those that a mesh axis runs over, the one named last changes fastest.
Arguments:
- acts: bfloat16 [65536, 2048], P(('dp', 'fsdp')), may hold values from -6 to 6
- grad_out: bfloat16 [65536, 2048], P(('dp', 'fsdp')), may hold values from -60 to 60
- weight: bfloat16 [2048, 2048], P('fsdp'), may hold values from -0.125 to 0.125
- basis: bfloat16 [2048, 512], P('fsdp'), may hold values from -3 to 3
- first_moment: float32 [512, 2048], P(('dp', 'fsdp')), may hold values from -4 to 4
- second_moment: float32 [512, 2048], P(('dp', 'fsdp')), may hold values from 0.0001 to 0.01
Outputs:
- grad_in: bfloat16 [65536, 2048], P(('dp', 'fsdp'))
- first_new: float32 [512, 2048], P(('dp', 'fsdp'))
- second_new: float32 [512, 2048], P(('dp', 'fsdp'))
- weight_update: bfloat16 [2048, 2048], P('fsdp')
The draws below stay inside these ranges and needn't reach their ends.
All inputs are finite; a program needn't handle non-finite values.
Results may differ from the reference program's by a relative error of at most 0.0056.
Values may be sent and summed in bfloat16 or wider, within the bound.
No kernel may reach another device: no remote copies, remote signals or barrier semaphores. Data moves between devices by JAX's collectives and lax.ppermute only.
A program may use at most 64 MiB of HBM per device.

```python
import math
import jax
import jax.numpy as jnp

D_IN = 2048
D_OUT = 2048
RANK = 512
TOKENS = 65536


def draw_grad_out(key, part):
    key = jax.random.fold_in(key, 11)
    noise_key, scale_key = jax.random.split(key, 2)
    column_scale = jnp.exp(jax.random.uniform(scale_key, (D_OUT,), jnp.float32, 0.0, math.log(10.0)))
    noise = jnp.clip(jax.random.normal(noise_key, (TOKENS, D_OUT), jnp.float32), -6.0, 6.0)
    values = noise * column_scale[None, :]
    return values.astype(jnp.bfloat16)


def draw_basis(key, part):
    key = jax.random.fold_in(key, 23)
    noise_key, scale_key = jax.random.split(key, 2)
    ladder = jnp.exp(jnp.arange(RANK, dtype=jnp.float32) * (math.log(10.0) / max(RANK - 1, 1)))
    jitter = jnp.exp(jax.random.uniform(scale_key, (RANK,), jnp.float32, 0.0, math.log(2.0)))
    column_scale = ladder * jitter / math.sqrt(D_IN)
    noise = jnp.clip(jax.random.normal(noise_key, (D_IN, RANK), jnp.float32), -5.0, 5.0)
    return (noise * column_scale[None, :]).astype(jnp.bfloat16)


def levels(rng, shape, cuts, least, largest):
    loudness, own = 1.0, jax.random.fold_in(rng, 6)
    for axis_at, parts in cuts:
        heights = jnp.exp(jax.random.uniform(jax.random.fold_in(own, axis_at), (parts,), jnp.float32, least / len(cuts), largest / len(cuts)))
        loudness = loudness * jnp.repeat(heights, shape[axis_at] // parts).reshape([-1 if axis == axis_at else 1 for axis in range(len(shape))])
    return loudness


def normal_values(stream_key, shape, scale, reach, cuts=(), kind=jnp.bfloat16):
    level = levels(stream_key, shape, cuts, -0.22, 0.18) if cuts else 1.0
    result = jax.random.normal(stream_key, shape, jnp.float32) * scale * level
    return jnp.minimum(jnp.maximum(result, -reach), reach).astype(kind)


def setup_inputs(seed: int = 0) -> dict:
    arg_keys = jax.random.split(jax.random.key(seed), 7)
    acts = normal_values(arg_keys[0], (TOKENS, D_IN), 1.0, 6.0, ((0, 512),))
    grad_out = draw_grad_out(jax.random.fold_in(arg_keys[6], 71), 0)
    weight = normal_values(arg_keys[2], (D_IN, D_OUT), D_IN ** -0.5, 0.125, ((0, 8),))
    basis = draw_basis(jax.random.fold_in(arg_keys[6], 71), 0)
    first_moment = normal_values(arg_keys[4], (RANK, D_OUT), 0.3, 4.0, ((0, 512),), jnp.float32)
    second_moment = jnp.clip(jnp.exp(math.log(0.01) - 4.6051702 * jax.random.uniform(arg_keys[5], (RANK, D_OUT), jnp.float32) ** levels(arg_keys[5], (RANK, D_OUT), ((0, 512),), -0.2, 0.2)), 0.0001, 0.01)
    return dict(acts=acts, grad_out=grad_out, weight=weight, basis=basis, first_moment=first_moment, second_moment=second_moment)


first_bias = 1.0 - 0.9 ** 10
second_bias = 1.0 - 0.999 ** 10

def reference(acts, grad_out, weight, basis, first_moment, second_moment):
    grad_in = jnp.dot(grad_out, weight.T, preferred_element_type=jnp.float32).astype(jnp.bfloat16)
    coords = jnp.dot(acts, basis, preferred_element_type=jnp.float32).astype(jnp.bfloat16)
    projected = jnp.dot(coords.T, grad_out, preferred_element_type=jnp.float32)
    total = jnp.sum(projected * projected)
    limit = math.sqrt(RANK * D_OUT)
    factor = jnp.minimum(1.0, limit / (jnp.sqrt(total) + 1e-06))
    clipped = factor * projected
    first_new = 0.9 * first_moment + 0.1 * clipped
    second_new = 0.999 * second_moment + 0.001 * clipped * clipped
    direction = (first_new / first_bias / (jnp.sqrt(second_new / second_bias) + 1e-08)).astype(jnp.bfloat16)
    update = jnp.dot(basis, direction, preferred_element_type=jnp.float32)
    weight_update = (0.25 * update).astype(jnp.bfloat16)
    return (grad_in, first_new, second_new, weight_update)
```

```python
import math

import jax
import jax.numpy as jnp
from jax import lax
from jax.sharding import Mesh
from jax.sharding import PartitionSpec as P

D_OUT = 2048
RANK = 512
AXES = ("yl", "z", "c", "yh", "x")
YX = ("yl", "yh", "x")
FSDP = ("yh", "x")
bf16 = jnp.bfloat16
f32 = jnp.float32

first_bias = 1.0 - 0.9**10
second_bias = 1.0 - 0.999**10


def spread(a, axes, peers):
    return lax.all_to_all(
        jnp.broadcast_to(a[None], (peers,) + a.shape), axes, 0, 0, tiled=True
    )


def adam(p, m, v, factor):
    clipped = factor * p
    first_new = 0.9 * m + 0.1 * clipped
    second_new = 0.999 * v + 0.001 * clipped * clipped
    return first_new, second_new


def on_device(acts, grad_out, weight, basis, first_moment, second_moment):
    core = lax.axis_index("c")
    swap = [(0, 1), (1, 0)]

    def other(a):
        return lax.ppermute(a, "c", swap)

    with jax.named_scope("pick"):
        col = lax.broadcasted_iota(jnp.int32, (RANK, RANK), 1)
        row = lax.broadcasted_iota(jnp.int32, (RANK, RANK), 0)
        own = jnp.where(col < 256, core, 1 - core)
        z, x, yh, yl = col % 16, (col // 16) % 4, (col // 64) % 2, (col // 128) % 2
        pick = (row == (((yl * 16 + z) * 2 + own) * 2 + yh) * 4 + x).astype(bf16)
        basis_p = jnp.dot(basis, pick, preferred_element_type=f32).astype(bf16)
    with jax.named_scope("swap_tokens"):
        acts2 = jnp.concatenate([acts, other(acts)], 0)
        grad2 = jnp.concatenate([grad_out, other(grad_out)], 0)
    with jax.named_scope("basis"):
        basis_all = spread(basis_p[:, :256], FSDP, 8).reshape(2048, 256)
    with jax.named_scope("weight"):
        half = lax.dynamic_slice_in_dim(weight, core * 128, 128, 0)
        weight_half = lax.all_gather(half, FSDP, axis=0, tiled=True)
    with jax.named_scope("projected"):
        coords = jnp.dot(acts2, basis_all, preferred_element_type=f32).astype(bf16)
        part = lax.dot_general(
            coords, grad2, (((0,), (0,)), ((), ())), preferred_element_type=f32
        ).astype(bf16)
    with jax.named_scope("sum_yx"):
        part = lax.all_to_all(part.reshape(16, 16, D_OUT), YX, 0, 0, tiled=True)
        part = jnp.sum(part.astype(f32), 0)
    with jax.named_scope("sum_z"):
        part = lax.all_to_all(part.reshape(16, 16, 128), "z", 0, 0, tiled=True)
        p = jnp.sum(part, 0)
    m = first_moment.reshape(16, 128)
    v = second_moment.reshape(16, 128)
    with jax.named_scope("rows_z"):
        rows = spread(jnp.concatenate([p, m, v], 0), "z", 16)
        p16, m16, v16 = rows[:, :16], rows[:, 16:32], rows[:, 32:]
    with jax.named_scope("total"):
        own = jnp.broadcast_to(jnp.sum(p16 * p16), (32, 128))
        sums = lax.all_to_all(own, ("yl", "c", "yh", "x"), 0, 0, tiled=True)
        total = jnp.sum(sums[:, 0])
        limit = math.sqrt(RANK * D_OUT)
        factor = jnp.minimum(1.0, limit / (jnp.sqrt(total) + 1e-06))
    with jax.named_scope("adam"):
        first_new, second_new = adam(p, m, v, factor)
        f16, s16 = adam(p16, m16, v16, factor)
        direction = (f16 / first_bias / (jnp.sqrt(s16 / second_bias) + 1e-08)).astype(bf16)
        direction = direction.reshape(16, D_OUT)
    with jax.named_scope("rows_yx"):
        mine = spread(direction, YX, 16).reshape(256, D_OUT)
    with jax.named_scope("update"):
        theirs = other(mine)
        update = jnp.dot(basis_p[:, :256], mine, preferred_element_type=f32)
        update = update + jnp.dot(basis_p[:, 256:], theirs, preferred_element_type=f32)
        weight_update = (0.25 * update).astype(bf16)
    with jax.named_scope("grad_in"):
        both = lax.dot_general(
            grad2, weight_half, (((1,), (1,)), ((), ())), preferred_element_type=f32
        ).astype(bf16)
        here, there = both[:128], other(both[128:])
        low = jnp.where(core == 0, here, there)
        high = jnp.where(core == 0, there, here)
        parts = []
        for k in range(8):
            parts += [low[:, k * 128 : k * 128 + 128], high[:, k * 128 : k * 128 + 128]]
        grad_in = jnp.concatenate(parts, 1)
    return (
        grad_in,
        first_new.reshape(1, D_OUT),
        second_new.reshape(1, D_OUT),
        weight_update,
    )


def solution(mesh):
    fine = Mesh(mesh.devices.reshape(2, 16, 2, 2, 4), AXES)
    rows = P(AXES, None)
    shared = P(FSDP, None)
    return jax.shard_map(
        on_device,
        mesh=fine,
        in_specs=(rows, rows, shared, shared, rows, rows),
        out_specs=(rows, rows, rows, shared),
        check_vma=False,
    )
```

```python
import math

import jax
import jax.numpy as jnp
from jax import lax
from jax.experimental import pallas as pl
from jax.experimental.pallas import tpu as pltpu
from jax.sharding import Mesh
from jax.sharding import PartitionSpec as P

D_OUT = 2048
RANK = 512
AXES = ("yl", "z", "c", "yh", "x")
YX = ("yl", "yh", "x")
FSDP = ("yh", "x")
bf16 = jnp.bfloat16
f32 = jnp.float32

first_bias = 1.0 - 0.9**10
second_bias = 1.0 - 0.999**10

ANY = pl.BlockSpec(memory_space=pl.ANY)
VMEM = pl.BlockSpec(memory_space=pltpu.VMEM)
SHORT = pl.CostEstimate(flops=1000, bytes_accessed=1000, transcendentals=0)
LONG = pl.CostEstimate(flops=20_000_000_000, bytes_accessed=1 << 20, transcendentals=0)


def shape(*dims, dtype=bf16):
    return jax.ShapeDtypeStruct(dims, dtype)


def call(body, outs, *args, first=None, cost=LONG):
    specs = [VMEM] * len(args)
    if first is not None:
        args, specs = (first,) + args, [ANY] + specs
    return pl.pallas_call(
        body,
        out_shape=outs,
        in_specs=specs,
        out_specs=(VMEM,) * len(outs) if isinstance(outs, tuple) else VMEM,
        compiler_params=pltpu.CompilerParams(vmem_limit_bytes=32 << 20),
        cost_estimate=cost,
    )(*args)


def half_kernel(_, w_ref, o_ref):
    start = pl.multiple_of(lax.axis_index("c") * 128, 128)
    o_ref[...] = w_ref[pl.ds(start, 128)]


def stack_kernel(_, a_ref, b_ref, o_ref):
    o_ref[:128] = a_ref[...]
    o_ref[128:] = b_ref[...]


def cut_kernel(_, a_ref, b_ref, lower_ref, upper_ref):
    lower_ref[...] = a_ref[:128]
    upper_ref[...] = b_ref[128:]


def backward_kernel(_, grad_ref, other_ref, pair, left, right, lower, upper, here, there):
    y, x = lax.axis_index("yh"), lax.axis_index("x")
    blocks = [(pair, 0, 0, 0), (pair, 1, 1, 0), (left, 0, 0, 3), (left, 1, 1, 3)]
    blocks += [(right, 0, 0, 1), (right, 1, 1, 1), (lower, 0, 0, 2), (upper, 0, 1, 2)]
    for ref, part, dy, dx in blocks:
        block = ((y + dy) % 2) * 4 + (x + dx) % 4
        at = pl.ds(pl.multiple_of(block * 128, 128), 128)
        w = ref[part * 128 : part * 128 + 128]
        for g_ref, o_ref in ((grad_ref, here), (other_ref, there)):
            o_ref[:, at] = lax.dot_general(
                g_ref[...], w, (((1,), (1,)), ((), ())), preferred_element_type=f32
            ).astype(bf16)


def weave_kernel(here_ref, there_ref, out_ref):
    core = lax.axis_index("c")
    for k in range(8):
        at = pl.ds(k * 128, 128)
        mine = pl.ds(pl.multiple_of(k * 256 + core * 128, 128), 128)
        theirs = pl.ds(pl.multiple_of(k * 256 + 128 - core * 128, 128), 128)
        out_ref[:, mine] = here_ref[:, at]
        out_ref[:, theirs] = there_ref[:, at]


def sum_yx_kernel(in_ref, out_ref):
    for j in range(16):
        at = pl.ds(j * 128, 128)
        acc = in_ref[0, :, at].astype(f32)
        for k in range(1, 16):
            acc += in_ref[k, :, at].astype(f32)
        out_ref[:, j, :] = acc


def sum_z_kernel(in_ref, m_ref, v_ref, p_ref, out_ref):
    p = jnp.sum(in_ref[...], 0)
    m, v = m_ref[...], v_ref[...]
    p_ref[...] = p
    for k in range(16):
        out_ref[k, :16] = p
        out_ref[k, 16:32] = m
        out_ref[k, 32:] = v


def squares_kernel(rows_ref, out_ref):
    p = rows_ref[:, :16]
    out_ref[...] = jnp.full((32, 128), jnp.sum(p * p), f32)


def adam(p, m, v, factor):
    clipped = factor * p
    first_new = 0.9 * m + 0.1 * clipped
    second_new = 0.999 * v + 0.001 * clipped * clipped
    return first_new, second_new


def adam_kernel(sums_ref, rows_ref, p_ref, m_ref, v_ref, out_ref, first_ref, second_ref):
    total = jnp.sum(sums_ref[...], 0, keepdims=True)
    limit = math.sqrt(RANK * D_OUT)
    factor = jnp.minimum(1.0, limit / (jnp.sqrt(total) + 1e-06))
    first_ref[...], second_ref[...] = adam(p_ref[...], m_ref[...], v_ref[...], factor)
    for j in range(16):
        p, m, v = (rows_ref[:, 16 * t + j, :] for t in range(3))
        f, s = adam(p, m, v, factor)
        d = (f / first_bias / (jnp.sqrt(s / second_bias) + 1e-08)).astype(bf16)
        for k in range(16):
            out_ref[k, :, pl.ds(j * 128, 128)] = d


def spread(a, axes, peers):
    return exchange(jnp.broadcast_to(a[None], (peers,) + a.shape), axes)


def exchange(a, axes):
    return lax.all_to_all(a, axes, 0, 0, tiled=True)


def shift(a, k):
    return lax.ppermute(a, "x", [(i, (i + k) % 4) for i in range(4)])


def on_device(acts, grad_out, weight, basis, first_moment, second_moment):
    core = lax.axis_index("c")
    swap = [(0, 1), (1, 0)]

    def other(a):
        return lax.ppermute(a, "c", swap)

    with jax.named_scope("pick"):
        col = lax.broadcasted_iota(jnp.int32, (RANK, RANK), 1)
        row = lax.broadcasted_iota(jnp.int32, (RANK, RANK), 0)
        own = jnp.where(col < 256, core, 1 - core)
        z, x, yh, yl = col % 16, (col // 16) % 4, (col // 64) % 2, (col // 128) % 2
        pick = (row == (((yl * 16 + z) * 2 + own) * 2 + yh) * 4 + x).astype(bf16)
        basis_p = jnp.dot(basis, pick, preferred_element_type=f32).astype(bf16)
    with jax.named_scope("swap_tokens"):
        grad_other = other(grad_out)
        acts2 = jnp.concatenate([acts, other(acts)], 0)
        grad2 = jnp.concatenate([grad_out, grad_other], 0)
    with jax.named_scope("basis"):
        basis_all = spread(basis_p[:, :256], FSDP, 8).reshape(2048, 256)
    with jax.named_scope("projected"):
        coords = jnp.dot(acts2, basis_all, preferred_element_type=f32).astype(bf16)
        part = lax.dot_general(
            coords, grad2, (((0,), (0,)), ((), ())), preferred_element_type=f32
        ).astype(bf16)
    with jax.named_scope("weight_y"):
        half = call(half_kernel, shape(128, 2048), weight, first=part)
        cross = lax.ppermute(half, "yh", swap)
    with jax.named_scope("sum_yx"):
        part = exchange(part.reshape(16, 16, D_OUT), YX)
        part, half = lax.optimization_barrier((part, half))
        part = call(sum_yx_kernel, shape(16, 16, 128, dtype=f32), part)
    with jax.named_scope("weight_x"):
        pair = call(stack_kernel, shape(256, 2048), half, cross, first=part)
        left, right = shift(pair, 1), shift(pair, 3)
    with jax.named_scope("sum_z"):
        part = exchange(part, "z")
        part, pair = lax.optimization_barrier((part, pair))
    m = first_moment.reshape(16, 128)
    v = second_moment.reshape(16, 128)
    with jax.named_scope("rows_z"):
        p, rows = call(
            sum_z_kernel,
            (shape(16, 128, dtype=f32), shape(16, 48, 128, dtype=f32)),
            part, m, v,
        )
    with jax.named_scope("weight_far"):
        low, high = call(cut_kernel, (shape(128, 2048),) * 2, left, right, first=p)
        lower, upper = shift(low, 1), shift(high, 3)
    with jax.named_scope("rows_z"):
        rows = exchange(rows, "z")
        rows, low, high = lax.optimization_barrier((rows, low, high))
    with jax.named_scope("total"):
        sums = exchange(call(squares_kernel, shape(32, 128, dtype=f32), rows), ("yl", "c", "yh", "x"))
    with jax.named_scope("adam"):
        direction, first_new, second_new = call(
            adam_kernel,
            (shape(16, 16, D_OUT), shape(16, 128, dtype=f32), shape(16, 128, dtype=f32)),
            sums, rows, p, m, v,
        )
    with jax.named_scope("grad_in"):
        here, there = call(
            backward_kernel,
            (shape(128, 1024),) * 2,
            grad_out, grad_other, pair, left, right, lower, upper,
            first=direction,
        )
        grad_in = call(weave_kernel, shape(128, D_OUT), here, other(there), cost=SHORT)
    with jax.named_scope("rows_yx"):
        mine = exchange(direction, YX).reshape(256, D_OUT)
        mine, grad_in = lax.optimization_barrier((mine, grad_in))
    with jax.named_scope("update"):
        theirs = other(mine)
        update = jnp.dot(basis_p[:, :256], mine, preferred_element_type=f32)
        update = update + jnp.dot(basis_p[:, 256:], theirs, preferred_element_type=f32)
        weight_update = (0.25 * update).astype(bf16)
    return (
        grad_in,
        first_new.reshape(1, D_OUT),
        second_new.reshape(1, D_OUT),
        weight_update,
    )


def solution(mesh):
    fine = Mesh(mesh.devices.reshape(2, 16, 2, 2, 4), AXES)
    rows = P(AXES, None)
    shared = P(FSDP, None)
    return jax.shard_map(
        on_device,
        mesh=fine,
        in_specs=(rows, rows, shared, shared, rows, rows),
        out_specs=(rows, rows, rows, shared),
        check_vma=False,
    )
```

```python
import math

import jax
import jax.numpy as jnp
from jax import lax
from jax.experimental import pallas as pl
from jax.experimental.pallas import tpu as pltpu
from jax.sharding import Mesh
from jax.sharding import PartitionSpec as P

D_OUT = 2048
RANK = 512
AXES = ("yl", "z", "c", "yh", "x")
YX = ("yl", "yh", "x")
FSDP = ("yh", "x")
bf16 = jnp.bfloat16
f32 = jnp.float32

first_bias = 1.0 - 0.9**10
second_bias = 1.0 - 0.999**10

ANY = pl.BlockSpec(memory_space=pl.ANY)
VMEM = pl.BlockSpec(memory_space=pltpu.VMEM)
SHORT = pl.CostEstimate(flops=1000, bytes_accessed=1000, transcendentals=0)
LONG = pl.CostEstimate(flops=20_000_000_000, bytes_accessed=1 << 20, transcendentals=0)


def shape(*dims, dtype=bf16):
    return jax.ShapeDtypeStruct(dims, dtype)


def call(body, outs, *args, first=None, cost=LONG, scratch=()):
    specs = [VMEM] * len(args)
    if first is not None:
        args, specs = (first,) + args, [ANY] + specs
    return pl.pallas_call(
        body,
        out_shape=outs,
        in_specs=specs,
        out_specs=(VMEM,) * len(outs) if isinstance(outs, tuple) else VMEM,
        compiler_params=pltpu.CompilerParams(vmem_limit_bytes=32 << 20),
        scratch_shapes=scratch,
        cost_estimate=cost,
    )(*args)


def picked(basis, core):
    col = lax.broadcasted_iota(jnp.int32, (1, 256), 1)
    z, x, yh, yl = col % 16, (col // 16) % 4, (col // 64) % 2, col // 128
    want = (((yl * 16 + z) * 2 + core) * 2 + yh) * 4 + x
    row = lax.broadcasted_iota(jnp.int32, (RANK, 256), 0)
    pick = jnp.where(row == want, 1.0, 0.0).astype(bf16)
    return jnp.dot(basis, pick, preferred_element_type=f32).astype(bf16)


def pick_own_kernel(basis_ref, own_ref, sent_ref):
    own = picked(basis_ref[...], lax.axis_index("c"))
    own_ref[...] = own
    for k in range(8):
        sent_ref[k] = own


def pick_other_kernel(_, basis_ref, out_ref):
    out_ref[...] = picked(basis_ref[...], 1 - lax.axis_index("c"))


def update_own_kernel(basis_ref, rows_ref, out_ref):
    for k in range(4):
        at = pl.ds(k * 512, 512)
        out_ref[:, at] = jnp.dot(
            basis_ref[...], rows_ref[:, at], preferred_element_type=f32
        )


def update_kernel(own_ref, basis_ref, rows_ref, out_ref):
    at = pl.ds(pl.multiple_of(pl.program_id(0) * 512, 512), 512)
    update = own_ref[:, at] + jnp.dot(
        basis_ref[...], rows_ref[:, at], preferred_element_type=f32
    )
    out_ref[...] = (0.25 * update).astype(bf16)


def half_kernel(_, w_ref, o_ref):
    start = pl.multiple_of(lax.axis_index("c") * 128, 128)
    o_ref[...] = w_ref[pl.ds(start, 128)]


def stack_kernel(_, a_ref, b_ref, o_ref):
    o_ref[:128] = a_ref[...]
    o_ref[128:] = b_ref[...]


def cut_kernel(_, a_ref, b_ref, lower_ref, upper_ref):
    lower_ref[...] = a_ref[:128]
    upper_ref[...] = b_ref[128:]


def blocks_of(refs, places):
    y, x = lax.axis_index("yh"), lax.axis_index("x")
    for ref, dy, dx in zip(refs, *places, strict=True):
        block = ((y + dy) % 2) * 4 + (x + dx) % 4
        yield pl.ds(pl.multiple_of(block * 128, 128), 128), ref


NEAR = ((0, 1, 0, 1, 0, 1), (0, 0, 3, 3, 1, 1))
FAR = ((0, 1), (2, 2))


def multiply(pairs, blocks):
    for at, ref in blocks:
        w = ref[...]
        for g_ref, o_ref in pairs:
            o_ref[:, at] = lax.dot_general(
                g_ref[...], w, (((1,), (1,)), ((), ())), preferred_element_type=f32
            ).astype(bf16)


def near_kernel(_, grad_ref, other_ref, pair, left, right, here, there):
    refs = [r.at[pl.ds(k * 128, 128)] for r in (pair, left, right) for k in range(2)]
    multiply(((grad_ref, here), (other_ref, there)), blocks_of(refs, NEAR))


def far_kernel(near_here, near_there, grad_ref, other_ref, lower, upper, here, there):
    for at, _ in blocks_of((None,) * 6, NEAR):
        here[:, at] = near_here[:, at]
        there[:, at] = near_there[:, at]
    multiply(((grad_ref, here), (other_ref, there)), blocks_of((lower, upper), FAR))


def weave_kernel(here_ref, there_ref, out_ref):
    core = lax.axis_index("c")
    for k in range(8):
        at = pl.ds(k * 128, 128)
        mine = pl.ds(pl.multiple_of(k * 256 + core * 128, 128), 128)
        theirs = pl.ds(pl.multiple_of(k * 256 + 128 - core * 128, 128), 128)
        out_ref[:, mine] = here_ref[:, at]
        out_ref[:, theirs] = there_ref[:, at]


def sum_yx_kernel(in_ref, out_ref):
    for j in range(16):
        at = pl.ds(j * 128, 128)
        acc = in_ref[0, :, at].astype(f32)
        for k in range(1, 16):
            acc += in_ref[k, :, at].astype(f32)
        out_ref[:, j, :] = acc


def sum_z_kernel(in_ref, m_ref, v_ref, p_ref, out_ref):
    p = jnp.sum(in_ref[...], 0)
    m, v = m_ref[...], v_ref[...]
    p_ref[...] = p
    for k in range(16):
        for t, row in enumerate((p, m, v)):
            out_ref[k, 16 * t : 16 * t + 16] = row.astype(bf16)


def squares_kernel(rows_ref, out_ref):
    p = rows_ref[:, :16].astype(f32)
    out_ref[...] = jnp.full((32, 128), jnp.sum(p * p), f32)


def adam(p, m, v, factor):
    clipped = factor * p
    first_new = 0.9 * m + 0.1 * clipped
    second_new = 0.999 * v + 0.001 * clipped * clipped
    return first_new, second_new


def adam_kernel(sums_ref, rows_ref, p_ref, m_ref, v_ref, out_ref, first_ref, second_ref, wide_ref):
    total = jnp.sum(sums_ref[...], 0, keepdims=True)
    limit = math.sqrt(RANK * D_OUT)
    factor = jnp.minimum(1.0, limit / (jnp.sqrt(total) + 1e-06))
    first_ref[...], second_ref[...] = adam(p_ref[...], m_ref[...], v_ref[...], factor)
    wide_ref[...] = rows_ref[...].astype(f32)
    for j in range(16):
        p, m, v = (wide_ref[:, 16 * t + j, :] for t in range(3))
        f, s = adam(p, m, v, factor)
        d = (f / first_bias / (jnp.sqrt(s / second_bias) + 1e-08)).astype(bf16)
        for k in range(16):
            out_ref[k, :, pl.ds(j * 128, 128)] = d


def exchange(a, axes):
    return lax.all_to_all(a, axes, 0, 0, tiled=True)


def shift(a, k):
    return lax.ppermute(a, "x", [(i, (i + k) % 4) for i in range(4)])


def on_device(acts, grad_out, weight, basis, first_moment, second_moment):
    core = lax.axis_index("c")
    swap = [(0, 1), (1, 0)]

    def other(a):
        return lax.ppermute(a, "c", swap)

    with jax.named_scope("pick"):
        basis_own, basis_sent = call(
            pick_own_kernel, (shape(256, 256), shape(8, 256, 256)), basis
        )
    with jax.named_scope("swap_tokens"):
        grad_other = other(grad_out)
        acts2 = jnp.concatenate([acts, other(acts)], 0)
        grad2 = jnp.concatenate([grad_out, grad_other], 0)
    with jax.named_scope("basis"):
        basis_all = exchange(basis_sent, FSDP).reshape(2048, 256)
    with jax.named_scope("projected"):
        coords = jnp.dot(acts2, basis_all, preferred_element_type=f32).astype(bf16)
        part = lax.dot_general(
            coords, grad2, (((0,), (0,)), ((), ())), preferred_element_type=f32
        ).astype(bf16)
        basis_other = call(pick_other_kernel, shape(256, 256), basis, first=part)
    with jax.named_scope("weight_y"):
        half = call(half_kernel, shape(128, 2048), weight, first=part)
        cross = lax.ppermute(half, "yh", swap)
    with jax.named_scope("sum_yx"):
        part = exchange(part.reshape(16, 16, D_OUT), YX)
        part, half = lax.optimization_barrier((part, half))
        part = call(sum_yx_kernel, shape(16, 16, 128, dtype=f32), part)
    with jax.named_scope("weight_x"):
        pair = call(stack_kernel, shape(256, 2048), half, cross, first=part)
        left, right = shift(pair, 1), shift(pair, 3)
    with jax.named_scope("sum_z"):
        part = exchange(part, "z")
        part, pair = lax.optimization_barrier((part, pair))
    m = first_moment.reshape(16, 128)
    v = second_moment.reshape(16, 128)
    with jax.named_scope("rows_z"):
        p, rows = call(
            sum_z_kernel,
            (shape(16, 128, dtype=f32), shape(16, 48, 128)),
            part, m, v,
        )
    with jax.named_scope("rows_z"):
        rows = exchange(rows, "z")
    with jax.named_scope("total"):
        sums = call(squares_kernel, shape(32, 128, dtype=f32), rows, cost=SHORT)
    with jax.named_scope("weight_far"):
        low, high = call(cut_kernel, (shape(128, 2048),) * 2, left, right, first=sums, cost=SHORT)
        lower, upper = shift(low, 1), shift(high, 3)
    with jax.named_scope("total"):
        sums = exchange(sums, ("yl", "c", "yh", "x"))
        sums, low, high = lax.optimization_barrier((sums, low, high))
    with jax.named_scope("adam"):
        direction, first_new, second_new = call(
            adam_kernel,
            (shape(16, 16, D_OUT), shape(16, 128, dtype=f32), shape(16, 128, dtype=f32)),
            sums, rows, p, m, v,
            scratch=[pltpu.VMEM((16, 48, 128), f32)],
        )
    with jax.named_scope("grad_in"):
        out = (shape(128, 1024),) * 2
        near = call(
            near_kernel, out, grad_out, grad_other, pair, left, right, first=direction
        )
        here, there = call(
            far_kernel, out, *near, grad_out, grad_other, lower, upper, cost=SHORT
        )
        grad_in = call(weave_kernel, shape(128, D_OUT), here, other(there), cost=SHORT)
    with jax.named_scope("rows_yx"):
        mine = exchange(direction, YX).reshape(256, D_OUT)
        mine, grad_in = lax.optimization_barrier((mine, grad_in))
    with jax.named_scope("update"):
        theirs = other(mine)
        update = call(update_own_kernel, shape(256, D_OUT, dtype=f32), basis_own, mine)
        weight_update = pl.pallas_call(
            update_kernel,
            out_shape=shape(256, D_OUT),
            grid=(4,),
            in_specs=[VMEM] * 3,
            out_specs=pl.BlockSpec((256, 512), lambda i: (0, i)),
            compiler_params=pltpu.CompilerParams(vmem_limit_bytes=32 << 20),
            cost_estimate=SHORT,
        )(update, basis_other, theirs)
    return (
        grad_in,
        first_new.reshape(1, D_OUT),
        second_new.reshape(1, D_OUT),
        weight_update,
    )


def solution(mesh):
    fine = Mesh(mesh.devices.reshape(2, 16, 2, 2, 4), AXES)
    rows = P(AXES, None)
    shared = P(FSDP, None)
    return jax.shard_map(
        on_device,
        mesh=fine,
        in_specs=(rows, rows, shared, shared, rows, rows),
        out_specs=(rows, rows, rows, shared),
        check_vma=False,
    )
```

```python
import math

import jax
import jax.numpy as jnp
from jax import lax
from jax.experimental import pallas as pl
from jax.experimental.pallas import tpu as pltpu
from jax.sharding import Mesh
from jax.sharding import PartitionSpec as P

D_OUT = 2048
RANK = 512
AXES = ("yl", "z", "c", "yh", "x")
YX = ("yl", "yh", "x")
FSDP = ("yh", "x")
bf16 = jnp.bfloat16
f32 = jnp.float32

first_bias = 1.0 - 0.9**10
second_bias = 1.0 - 0.999**10

ANY = pl.BlockSpec(memory_space=pl.ANY)
VMEM = pl.BlockSpec(memory_space=pltpu.VMEM)
SHORT = pl.CostEstimate(flops=1000, bytes_accessed=1000, transcendentals=0)
LONG = pl.CostEstimate(flops=20_000_000_000, bytes_accessed=1 << 20, transcendentals=0)


def shape(*dims, dtype=bf16):
    return jax.ShapeDtypeStruct(dims, dtype)


def call(body, outs, *args, first=None, cost=LONG, scratch=()):
    specs = [VMEM] * len(args)
    if first is not None:
        args, specs = (first,) + args, [ANY] + specs
    return pl.pallas_call(
        body,
        out_shape=outs,
        in_specs=specs,
        out_specs=(VMEM,) * len(outs) if isinstance(outs, tuple) else VMEM,
        compiler_params=pltpu.CompilerParams(vmem_limit_bytes=32 << 20),
        scratch_shapes=scratch,
        cost_estimate=cost,
    )(*args)


def picked(basis, core):
    col = lax.broadcasted_iota(jnp.int32, (1, 256), 1)
    z, x, yh, yl = col % 16, (col // 16) % 4, (col // 64) % 2, col // 128
    want = (((yl * 16 + z) * 2 + core) * 2 + yh) * 4 + x
    row = lax.broadcasted_iota(jnp.int32, (RANK, 256), 0)
    pick = jnp.where(row == want, 1.0, 0.0).astype(bf16)
    return jnp.dot(basis, pick, preferred_element_type=f32).astype(bf16)


def pick_own_kernel(basis_ref, own_ref, sent_ref):
    own = picked(basis_ref[...], lax.axis_index("c"))
    own_ref[...] = own
    for k in range(8):
        sent_ref[k] = own


def pick_other_kernel(_, basis_ref, out_ref):
    out_ref[...] = picked(basis_ref[...], 1 - lax.axis_index("c"))


def update_own_kernel(basis_ref, rows_ref, out_ref):
    for k in range(4):
        at = pl.ds(k * 512, 512)
        out_ref[:, at] = jnp.dot(
            basis_ref[...], rows_ref[:, at], preferred_element_type=f32
        )


def update_kernel(own_ref, basis_ref, rows_ref, out_ref):
    at = pl.ds(pl.multiple_of(pl.program_id(0) * 1024, 1024), 1024)
    update = own_ref[:, at] + jnp.dot(
        basis_ref[...], rows_ref[:, at], preferred_element_type=f32
    )
    out_ref[...] = (0.25 * update).astype(bf16)


def half_kernel(_, w_ref, o_ref):
    start = pl.multiple_of(lax.axis_index("c") * 128, 128)
    o_ref[...] = w_ref[pl.ds(start, 128)]


def stack_kernel(_, a_ref, b_ref, o_ref):
    o_ref[:128] = a_ref[...]
    o_ref[128:] = b_ref[...]


def choose_kernel(_, left_ref, right_ref, out_ref):
    @pl.when(lax.axis_index("c") == 0)
    def _():
        out_ref[...] = left_ref[...]

    @pl.when(lax.axis_index("c") == 1)
    def _():
        out_ref[...] = right_ref[...]


def blocks_of(refs, places):
    y, x = lax.axis_index("yh"), lax.axis_index("x")
    for ref, dy, dx in zip(refs, *places, strict=True):
        block = ((y + dy) % 2) * 4 + (x + dx) % 4
        yield pl.ds(pl.multiple_of(block * 128, 128), 128), ref


def halves(ref):
    return [ref.at[pl.ds(k * 128, 128)] for k in range(2)]


NEAR = ((0, 1, 0, 1, 0, 1), (0, 0, 3, 3, 1, 1))
FAR = ((0, 1), (2, 2))


def multiply(pairs, blocks):
    for at, ref in blocks:
        w = ref[...]
        for g_ref, o_ref in pairs:
            o_ref[:, at] = lax.dot_general(
                g_ref[...], w, (((1,), (1,)), ((), ())), preferred_element_type=f32
            ).astype(bf16)


def near_kernel(_, grad_ref, other_ref, pair, left, right, here, there):
    refs = halves(pair) + halves(left) + halves(right)
    multiply(((grad_ref, here), (other_ref, there)), blocks_of(refs, NEAR))


def far_kernel(near_here, near_there, grad_ref, other_ref, far, here, there):
    for at, _ in blocks_of((None,) * 6, NEAR):
        here[:, at] = near_here[:, at]
        there[:, at] = near_there[:, at]
    multiply(((grad_ref, here), (other_ref, there)), blocks_of(halves(far), FAR))


def weave_kernel(here_ref, there_ref, out_ref):
    core = lax.axis_index("c")
    for k in range(8):
        at = pl.ds(k * 128, 128)
        mine = pl.ds(pl.multiple_of(k * 256 + core * 128, 128), 128)
        theirs = pl.ds(pl.multiple_of(k * 256 + 128 - core * 128, 128), 128)
        out_ref[:, mine] = here_ref[:, at]
        out_ref[:, theirs] = there_ref[:, at]


def sum_yx_kernel(in_ref, out_ref):
    for j in range(16):
        at = pl.ds(j * 128, 128)
        acc = in_ref[0, :, at].astype(f32)
        for k in range(1, 16):
            acc += in_ref[k, :, at].astype(f32)
        out_ref[:, j, :] = acc


def sum_z_kernel(in_ref, m_ref, v_ref, p_ref, out_ref):
    p = jnp.sum(in_ref[...], 0)
    m, v = m_ref[...], v_ref[...]
    p_ref[...] = p
    for k in range(16):
        for t, row in enumerate((p, m, v)):
            out_ref[k, 16 * t : 16 * t + 16] = row.astype(bf16)


def squares_kernel(rows_ref, out_ref):
    p = rows_ref[:, :16].astype(f32)
    out_ref[...] = jnp.full((32, 128), jnp.sum(p * p), f32)


def adam(p, m, v, factor):
    clipped = factor * p
    first_new = 0.9 * m + 0.1 * clipped
    second_new = 0.999 * v + 0.001 * clipped * clipped
    return first_new, second_new


def adam_kernel(sums_ref, rows_ref, p_ref, m_ref, v_ref, out_ref, first_ref, second_ref, wide_ref):
    total = jnp.sum(sums_ref[...], 0, keepdims=True)
    limit = math.sqrt(RANK * D_OUT)
    factor = jnp.minimum(1.0, limit / (jnp.sqrt(total) + 1e-06))
    first_ref[...], second_ref[...] = adam(p_ref[...], m_ref[...], v_ref[...], factor)
    wide_ref[...] = rows_ref[...].astype(f32)
    for j in range(16):
        p, m, v = (wide_ref[:, 16 * t + j, :] for t in range(3))
        f, s = adam(p, m, v, factor)
        d = (f / first_bias / (jnp.sqrt(s / second_bias) + 1e-08)).astype(bf16)
        for k in range(16):
            out_ref[k, :, pl.ds(j * 128, 128)] = d


def exchange(a, axes):
    return lax.all_to_all(a, axes, 0, 0, tiled=True)


def shift(a, k):
    return lax.ppermute(a, "x", [(i, (i + k) % 4) for i in range(4)])


def on_device(acts, grad_out, weight, basis, first_moment, second_moment):
    core = lax.axis_index("c")
    swap = [(0, 1), (1, 0)]

    def other(a):
        return lax.ppermute(a, "c", swap)

    with jax.named_scope("pick"):
        basis_own, basis_sent = call(
            pick_own_kernel, (shape(256, 256), shape(8, 256, 256)), basis
        )
    with jax.named_scope("swap_tokens"):
        grad_other = other(grad_out)
        acts2 = jnp.concatenate([acts, other(acts)], 0)
        grad2 = jnp.concatenate([grad_out, grad_other], 0)
    with jax.named_scope("basis"):
        basis_all = exchange(basis_sent, FSDP).reshape(2048, 256)
    with jax.named_scope("projected"):
        coords = jnp.dot(acts2, basis_all, preferred_element_type=f32).astype(bf16)
        part = lax.dot_general(
            coords, grad2, (((0,), (0,)), ((), ())), preferred_element_type=f32
        ).astype(bf16)
        basis_other = call(pick_other_kernel, shape(256, 256), basis, first=part)
    with jax.named_scope("weight_y"):
        half = call(half_kernel, shape(128, 2048), weight, first=part)
        cross = lax.ppermute(half, "yh", swap)
    with jax.named_scope("sum_yx"):
        part = exchange(part.reshape(16, 16, D_OUT), YX)
        part, half = lax.optimization_barrier((part, half))
        part = call(sum_yx_kernel, shape(16, 16, 128, dtype=f32), part)
    with jax.named_scope("weight_x"):
        pair = call(stack_kernel, shape(256, 2048), half, cross, first=part)
        left, right = shift(pair, 1), shift(pair, 3)
    with jax.named_scope("sum_z"):
        part = exchange(part, "z")
        part, pair = lax.optimization_barrier((part, pair))
    m = first_moment.reshape(16, 128)
    v = second_moment.reshape(16, 128)
    with jax.named_scope("rows_z"):
        p, rows = call(
            sum_z_kernel,
            (shape(16, 128, dtype=f32), shape(16, 48, 128)),
            part, m, v,
        )
    with jax.named_scope("rows_z"):
        rows = exchange(rows, "z")
    with jax.named_scope("total"):
        sums = call(squares_kernel, shape(32, 128, dtype=f32), rows, cost=SHORT)
    with jax.named_scope("weight_far"):
        passed = call(choose_kernel, shape(256, 2048), left, right, first=sums, cost=SHORT)
        onward = [(i, (i + 1) % 4) for i in range(4)]
        onward += [(4 + i, 4 + (i + 3) % 4) for i in range(4)]
        far = lax.ppermute(passed, ("c", "x"), onward)
    with jax.named_scope("total"):
        sums = exchange(sums, ("yl", "c", "yh", "x"))
        sums, passed = lax.optimization_barrier((sums, passed))
    with jax.named_scope("adam"):
        direction, first_new, second_new = call(
            adam_kernel,
            (shape(16, 16, D_OUT), shape(16, 128, dtype=f32), shape(16, 128, dtype=f32)),
            sums, rows, p, m, v,
            scratch=[pltpu.VMEM((16, 48, 128), f32)],
        )
    with jax.named_scope("grad_in"):
        out = (shape(128, 1024),) * 2
        near = call(
            near_kernel, out, grad_out, grad_other, pair, left, right, first=first_new
        )
        here, there = call(
            far_kernel, out, *near, grad_out, grad_other, far, cost=SHORT
        )
        grad_in = call(weave_kernel, shape(128, D_OUT), here, other(there), cost=SHORT)
    with jax.named_scope("rows_yx"):
        mine = exchange(direction, YX).reshape(256, D_OUT)
        mine, grad_in = lax.optimization_barrier((mine, grad_in))
    with jax.named_scope("update"):
        theirs = other(mine)
        update = call(update_own_kernel, shape(256, D_OUT, dtype=f32), basis_own, mine)
        weight_update = pl.pallas_call(
            update_kernel,
            out_shape=shape(256, D_OUT),
            grid=(2,),
            in_specs=[VMEM] * 3,
            out_specs=pl.BlockSpec((256, 1024), lambda i: (0, i)),
            compiler_params=pltpu.CompilerParams(vmem_limit_bytes=32 << 20),
            cost_estimate=SHORT,
        )(update, basis_other, theirs)
    return (
        grad_in,
        first_new.reshape(1, D_OUT),
        second_new.reshape(1, D_OUT),
        weight_update,
    )


def solution(mesh):
    fine = Mesh(mesh.devices.reshape(2, 16, 2, 2, 4), AXES)
    rows = P(AXES, None)
    shared = P(FSDP, None)
    return jax.shard_map(
        on_device,
        mesh=fine,
        in_specs=(rows, rows, shared, shared, rows, rows),
        out_specs=(rows, rows, rows, shared),
        check_vma=False,
    )
```

```python
import math

import jax
import jax.numpy as jnp
from jax import lax
from jax.experimental import pallas as pl
from jax.experimental.pallas import tpu as pltpu
from jax.sharding import Mesh
from jax.sharding import PartitionSpec as P

D_OUT = 2048
RANK = 512
AXES = ("yl", "z", "c", "yh", "x")
YX = ("yl", "yh", "x")
FSDP = ("yh", "x")
bf16 = jnp.bfloat16
f32 = jnp.float32

first_bias = 1.0 - 0.9**10
second_bias = 1.0 - 0.999**10

ANY = pl.BlockSpec(memory_space=pl.ANY)
VMEM = pl.BlockSpec(memory_space=pltpu.VMEM)
SHORT = pl.CostEstimate(flops=1000, bytes_accessed=1000, transcendentals=0)
LONG = pl.CostEstimate(flops=20_000_000_000, bytes_accessed=1 << 20, transcendentals=0)


def shape(*dims, dtype=bf16):
    return jax.ShapeDtypeStruct(dims, dtype)


def call(body, outs, *args, first=None, cost=LONG, scratch=()):
    specs = [VMEM] * len(args)
    if first is not None:
        args, specs = (first,) + args, [ANY] + specs
    return pl.pallas_call(
        body,
        out_shape=outs,
        in_specs=specs,
        out_specs=(VMEM,) * len(outs) if isinstance(outs, tuple) else VMEM,
        compiler_params=pltpu.CompilerParams(vmem_limit_bytes=32 << 20),
        scratch_shapes=scratch,
        cost_estimate=cost,
    )(*args)


def picked(basis, core):
    col = lax.broadcasted_iota(jnp.int32, (1, 256), 1)
    z, x, yh, yl = col % 16, (col // 16) % 4, (col // 64) % 2, col // 128
    want = (((yl * 16 + z) * 2 + core) * 2 + yh) * 4 + x
    row = lax.broadcasted_iota(jnp.int32, (RANK, 256), 0)
    pick = jnp.where(row == want, 1.0, 0.0).astype(bf16)
    return jnp.dot(basis, pick, preferred_element_type=f32).astype(bf16)


def pick_own_kernel(basis_ref, own_ref, sent_ref):
    own = picked(basis_ref[...], lax.axis_index("c"))
    own_ref[...] = own
    for k in range(8):
        sent_ref[k] = own


def pick_other_kernel(_, basis_ref, out_ref):
    out_ref[...] = picked(basis_ref[...], 1 - lax.axis_index("c"))


def update_own_kernel(basis_ref, rows_ref, out_ref):
    for k in range(4):
        at = pl.ds(k * 512, 512)
        out_ref[:, at] = jnp.dot(
            basis_ref[...], rows_ref[:, at], preferred_element_type=f32
        )


def update_kernel(own_ref, basis_ref, rows_ref, out_ref):
    at = pl.ds(pl.multiple_of(pl.program_id(0) * 1024, 1024), 1024)
    update = own_ref[:, at] + jnp.dot(
        basis_ref[...], rows_ref[:, at], preferred_element_type=f32
    )
    out_ref[...] = (0.25 * update).astype(bf16)


def projected_kernel(acts_ref, acts2_ref, grad_ref, grad2_ref, basis_ref, out_ref):
    basis = basis_ref[...]
    coords = [
        jnp.dot(a[...], basis, preferred_element_type=f32).T.astype(bf16)
        for a in (acts_ref, acts2_ref)
    ]
    for k in range(4):
        at = pl.ds(k * 512, 512)
        part = [
            jnp.dot(c, g[:, at], preferred_element_type=f32)
            for c, g in zip(coords, (grad_ref, grad2_ref), strict=True)
        ]
        out_ref[:, at] = (part[0] + part[1]).astype(bf16)


def half_kernel(_, w_ref, o_ref):
    start = pl.multiple_of(lax.axis_index("c") * 128, 128)
    o_ref[...] = w_ref[pl.ds(start, 128)]


def stack_kernel(_, a_ref, b_ref, o_ref):
    o_ref[:128] = a_ref[...]
    o_ref[128:] = b_ref[...]


def choose_kernel(_, left_ref, right_ref, out_ref):
    @pl.when(lax.axis_index("c") == 0)
    def _():
        out_ref[...] = left_ref[...]

    @pl.when(lax.axis_index("c") == 1)
    def _():
        out_ref[...] = right_ref[...]


def blocks_of(refs, places):
    y, x = lax.axis_index("yh"), lax.axis_index("x")
    for ref, dy, dx in zip(refs, *places, strict=True):
        block = ((y + dy) % 2) * 4 + (x + dx) % 4
        yield pl.ds(pl.multiple_of(block * 128, 128), 128), ref


def halves(ref):
    return [ref.at[pl.ds(k * 128, 128)] for k in range(2)]


NEAR = ((0, 1, 0, 1, 0, 1), (0, 0, 3, 3, 1, 1))
FAR = ((0, 1), (2, 2))


def multiply(pairs, blocks):
    for at, ref in blocks:
        w = ref[...]
        for g_ref, o_ref in pairs:
            o_ref[:, at] = lax.dot_general(
                g_ref[...], w, (((1,), (1,)), ((), ())), preferred_element_type=f32
            ).astype(bf16)


def near_kernel(_, grad_ref, other_ref, pair, left, right, here, there):
    refs = halves(pair) + halves(left) + halves(right)
    multiply(((grad_ref, here), (other_ref, there)), blocks_of(refs, NEAR))


def far_kernel(near_here, near_there, grad_ref, other_ref, far, here, there):
    for at, _ in blocks_of((None,) * 6, NEAR):
        here[:, at] = near_here[:, at]
        there[:, at] = near_there[:, at]
    multiply(((grad_ref, here), (other_ref, there)), blocks_of(halves(far), FAR))


def weave_kernel(here_ref, there_ref, out_ref):
    core = lax.axis_index("c")
    for k in range(8):
        at = pl.ds(k * 128, 128)
        mine = pl.ds(pl.multiple_of(k * 256 + core * 128, 128), 128)
        theirs = pl.ds(pl.multiple_of(k * 256 + 128 - core * 128, 128), 128)
        out_ref[:, mine] = here_ref[:, at]
        out_ref[:, theirs] = there_ref[:, at]


def sum_yx_kernel(in_ref, out_ref):
    for j in range(16):
        at = pl.ds(j * 128, 128)
        acc = in_ref[0, :, at].astype(f32)
        for k in range(1, 16):
            acc += in_ref[k, :, at].astype(f32)
        out_ref[:, j, :] = acc


def sum_z_kernel(in_ref, m_ref, v_ref, p_ref, out_ref):
    p = jnp.sum(in_ref[...], 0)
    m, v = m_ref[...], v_ref[...]
    p_ref[...] = p
    for k in range(16):
        for t, row in enumerate((p, m, v)):
            out_ref[k, 16 * t : 16 * t + 16] = row.astype(bf16)


def squares_kernel(rows_ref, out_ref):
    p = rows_ref[:, :16].astype(f32)
    out_ref[...] = jnp.full((32, 128), jnp.sum(p * p), f32)


def adam(p, m, v, factor):
    clipped = factor * p
    first_new = 0.9 * m + 0.1 * clipped
    second_new = 0.999 * v + 0.001 * clipped * clipped
    return first_new, second_new


def adam_kernel(sums_ref, rows_ref, p_ref, m_ref, v_ref, out_ref, first_ref, second_ref, wide_ref):
    total = jnp.sum(sums_ref[...], 0, keepdims=True)
    limit = math.sqrt(RANK * D_OUT)
    factor = jnp.minimum(1.0, limit / (jnp.sqrt(total) + 1e-06))
    first_ref[...], second_ref[...] = adam(p_ref[...], m_ref[...], v_ref[...], factor)
    wide_ref[...] = rows_ref[...].astype(f32)
    for j in range(16):
        p, m, v = (wide_ref[:, 16 * t + j, :] for t in range(3))
        f, s = adam(p, m, v, factor)
        d = (f / first_bias / (jnp.sqrt(s / second_bias) + 1e-08)).astype(bf16)
        for k in range(16):
            out_ref[k, :, pl.ds(j * 128, 128)] = d


def exchange(a, axes):
    return lax.all_to_all(a, axes, 0, 0, tiled=True)


def shift(a, k):
    return lax.ppermute(a, "x", [(i, (i + k) % 4) for i in range(4)])


def on_device(acts, grad_out, weight, basis, first_moment, second_moment):
    core = lax.axis_index("c")
    swap = [(0, 1), (1, 0)]

    def other(a):
        return lax.ppermute(a, "c", swap)

    with jax.named_scope("pick"):
        basis_own, basis_sent = call(
            pick_own_kernel, (shape(256, 256), shape(8, 256, 256)), basis
        )
    with jax.named_scope("swap_tokens"):
        grad_other = other(grad_out)
        acts_other = other(acts)
    with jax.named_scope("basis"):
        basis_all = exchange(basis_sent, FSDP).reshape(2048, 256)
    with jax.named_scope("projected"):
        part = call(
            projected_kernel,
            shape(256, D_OUT),
            acts, acts_other, grad_out, grad_other, basis_all,
        )
        basis_other = call(pick_other_kernel, shape(256, 256), basis, first=part)
    with jax.named_scope("weight_y"):
        half = call(half_kernel, shape(128, 2048), weight, first=part)
        cross = lax.ppermute(half, "yh", swap)
    with jax.named_scope("sum_yx"):
        part = exchange(part.reshape(16, 16, D_OUT), YX)
        part, half = lax.optimization_barrier((part, half))
        part = call(sum_yx_kernel, shape(16, 16, 128, dtype=f32), part)
    with jax.named_scope("weight_x"):
        pair = call(stack_kernel, shape(256, 2048), half, cross, first=part)
        left, right = shift(pair, 1), shift(pair, 3)
    with jax.named_scope("sum_z"):
        part = exchange(part, "z")
        part, pair = lax.optimization_barrier((part, pair))
    m = first_moment.reshape(16, 128)
    v = second_moment.reshape(16, 128)
    with jax.named_scope("rows_z"):
        p, rows = call(
            sum_z_kernel,
            (shape(16, 128, dtype=f32), shape(16, 48, 128)),
            part, m, v,
        )
    with jax.named_scope("rows_z"):
        rows = exchange(rows, "z")
    with jax.named_scope("total"):
        sums = call(squares_kernel, shape(32, 128, dtype=f32), rows, cost=SHORT)
    with jax.named_scope("weight_far"):
        passed = call(choose_kernel, shape(256, 2048), left, right, first=sums, cost=SHORT)
        onward = [(i, (i + 1) % 4) for i in range(4)]
        onward += [(4 + i, 4 + (i + 3) % 4) for i in range(4)]
        far = lax.ppermute(passed, ("c", "x"), onward)
    with jax.named_scope("total"):
        sums = exchange(sums, ("yl", "c", "yh", "x"))
        sums, passed = lax.optimization_barrier((sums, passed))
    with jax.named_scope("adam"):
        direction, first_new, second_new = call(
            adam_kernel,
            (shape(16, 16, D_OUT), shape(16, 128, dtype=f32), shape(16, 128, dtype=f32)),
            sums, rows, p, m, v,
            scratch=[pltpu.VMEM((16, 48, 128), f32)],
        )
    with jax.named_scope("grad_in"):
        out = (shape(128, 1024),) * 2
        near = call(
            near_kernel, out, grad_out, grad_other, pair, left, right, first=first_new
        )
        here, there = call(
            far_kernel, out, *near, grad_out, grad_other, far, cost=SHORT
        )
        grad_in = call(weave_kernel, shape(128, D_OUT), here, other(there), cost=SHORT)
    with jax.named_scope("rows_yx"):
        mine = exchange(direction, YX).reshape(256, D_OUT)
        mine, grad_in = lax.optimization_barrier((mine, grad_in))
    with jax.named_scope("update"):
        theirs = other(mine)
        update = call(update_own_kernel, shape(256, D_OUT, dtype=f32), basis_own, mine)
        weight_update = pl.pallas_call(
            update_kernel,
            out_shape=shape(256, D_OUT),
            grid=(2,),
            in_specs=[VMEM] * 3,
            out_specs=pl.BlockSpec((256, 1024), lambda i: (0, i)),
            compiler_params=pltpu.CompilerParams(vmem_limit_bytes=32 << 20),
            cost_estimate=SHORT,
        )(update, basis_other, theirs)
    return (
        grad_in,
        first_new.reshape(1, D_OUT),
        second_new.reshape(1, D_OUT),
        weight_update,
    )


def solution(mesh):
    fine = Mesh(mesh.devices.reshape(2, 16, 2, 2, 4), AXES)
    rows = P(AXES, None)
    shared = P(FSDP, None)
    return jax.shard_map(
        on_device,
        mesh=fine,
        in_specs=(rows, rows, shared, shared, rows, rows),
        out_specs=(rows, rows, rows, shared),
        check_vma=False,
    )
```
